32 devices in a mesh: segment: 4 (over y, x), dp: 8 (over z, core).
Axes of the slice: x: 2, y: 2, z: 4, core: 2. Of those that a mesh axis runs over, the one named last changes fastest.
Arguments:
- stem: bfloat16 [32, 6, 6, 512], P('dp'), may hold values from -6 to 6
- labels: int32 [32], P('dp'), may hold values from 0 to 999
- cell_count: int32 [4], P('segment'), may hold values from 1 to 2, as said below
- pointwise: bfloat16 [8, 2, 512, 512], P('segment'), may hold values from -0.25 to 0.25
- depth_three: bfloat16 [8, 9, 512], P('segment'), may hold values from -2 to 2
- depth_five: bfloat16 [8, 25, 512], P('segment'), may hold values from -1.25 to 1.25
- classifier: bfloat16 [512, 1000], replicated, may hold values from -0.25 to 0.25
Outputs:
- grad_pointwise: float32 [8, 2, 512, 512], P('segment', None, None, 'dp')
- grad_three: float32 [8, 9, 512], P('segment', None, 'dp')
- grad_five: float32 [8, 25, 512], P('segment', None, 'dp')
The draws below stay inside these ranges and needn't reach their ends.
Inputs may be any that keep to these rules, and one draw needn't show every extreme that they name: `cell_count`: some section runs 2 cells and some section runs one.
All inputs are finite; a program needn't handle non-finite values.
Results may differ from the reference program's by a relative error of at most 0.013.
Values may be sent and summed in bfloat16 or wider, within the bound.
No kernel may reach another device: no remote copies, remote signals or barrier semaphores. Data moves between devices by JAX's collectives and lax.ppermute only.
A program may use at most 128 MiB of HBM per device.

```python
import jax
import jax.numpy as jnp
from jax import lax

F = 512
CLASSES = 1000
SIDE = 6
MICRO = 4
SLOTS = 2
CELLS = 8
BATCH = 32
N_SEGMENT = 4
N_DP = 8


def draw_cell_count(key, part):
    key = jax.random.fold_in(key, 7)
    first, second = jax.random.split(key)
    counts = jax.random.randint(first, (N_SEGMENT,), 1, SLOTS + 1)
    order = jax.random.permutation(second, N_SEGMENT)
    counts = counts.at[order[0]].set(SLOTS).at[order[1]].set(1)
    return counts.astype(jnp.int32)


def set_ends(entries, own_key, low, top_value):
    index_at = [jax.random.randint(jax.random.fold_in(own_key, axis), (), 0, length) for axis, length in enumerate(entries.shape)]
    longest = entries.shape.index(max(entries.shape))
    beside = index_at[:longest] + [(index_at[longest] + 1) % entries.shape[longest]] + index_at[longest + 1:]
    return entries.at[tuple(index_at)].set(low).at[tuple(beside)].set(top_value)


def block_scale(own_key, extent, pieces, least, high):
    factor_of, own = 1.0, jax.random.fold_in(own_key, 6)
    for position, parts in pieces:
        steps = jnp.exp(jax.random.uniform(jax.random.fold_in(own, position), (parts,), jnp.float32, least / len(pieces), high / len(pieces)))
        factor_of = factor_of * jnp.repeat(steps, extent[position] // parts).reshape([-1 if axis == position else 1 for axis in range(len(extent))])
    return factor_of


def scatter_about(rng, dims, scale, bound, cuts=(), held_as=jnp.bfloat16):
    array = scale * jax.random.normal(rng, dims, jnp.float32)
    if cuts:
        array = array * block_scale(rng, dims, cuts, -0.22, 0.18)
    return jnp.clip(array, -bound, bound).astype(held_as)


def setup_inputs(seed: int = 0) -> dict:
    keys = jax.random.split(jax.random.key(seed), 8)
    return {
        "stem": scatter_about(keys[0], (BATCH, SIDE, SIDE, F), 1.0, 6.0, ((0, 8),)),
        "labels": set_ends(jax.random.randint(keys[1], (BATCH,), 0, CLASSES), jax.random.fold_in(keys[1], 1), 0, CLASSES - 1).astype(jnp.int32),
        "cell_count": draw_cell_count(jax.random.fold_in(keys[7], 71), 0),
        "pointwise": scatter_about(keys[3], (CELLS, 2, F, F), F ** -0.5, 0.25, ((0, 4),)),
        "depth_three": scatter_about(keys[4], (CELLS, 9, F), 9 ** -0.5, 2.0, ((0, 4),)),
        "depth_five": scatter_about(keys[5], (CELLS, 25, F), 25 ** -0.5, 1.25, ((0, 4),)),
        "classifier": scatter_about(keys[6], (F, CLASSES), F ** -0.5, 0.25),
    }


LOSS_SCALE = 256.0

def depthwise(image, taps, width):
    reach = width // 2
    side = image.shape[0]
    padded = jnp.pad(image.astype(jnp.float32), ((reach, reach), (reach, reach), (0, 0)))
    total = jnp.zeros(image.shape, jnp.float32)
    for row in range(width):
        for column in range(width):
            total = total + padded[row:row + side, column:column + side] * taps[row * width + column]
    return total

def cell(pair, weight_pw, weight_three, weight_five):
    older, newer = (pair[0], pair[1])
    side, feat = (newer.shape[0], newer.shape[2])
    zero = jnp.zeros((), newer.dtype)
    branch_a = lax.optimization_barrier(depthwise(jnp.maximum(newer, zero), weight_three, 3).astype(jnp.bfloat16))
    branch_b = lax.optimization_barrier(depthwise(jnp.maximum(older, zero), weight_five, 5).astype(jnp.bfloat16))
    left = jnp.dot(branch_a.astype(jnp.float32).reshape(-1, feat), weight_pw[0])
    right = jnp.dot(branch_b.astype(jnp.float32).reshape(-1, feat), weight_pw[1])
    fresh = (left + right).reshape(side, side, feat).astype(jnp.bfloat16)
    return jnp.stack([newer, fresh])

def segment_run(pair, weight_pw, weight_three, weight_five, count):
    for slot in range(weight_pw.shape[0]):
        pair = lax.cond(slot < count, lambda p, s=slot: cell(p, weight_pw[s], weight_three[s], weight_five[s]), lambda p: p, pair)
    return pair

def head_loss(final, classifier, label):
    pooled = lax.optimization_barrier(jnp.mean(final.astype(jnp.float32), axis=(0, 1)))
    logits = jnp.dot(pooled, classifier.astype(jnp.float32), precision=lax.Precision.HIGHEST)
    target = (jnp.arange(logits.shape[0], dtype=jnp.int32) == label).astype(jnp.float32)
    return 0.5 * LOSS_SCALE * jnp.sum((logits - target) ** 2)

def reference(stem, labels, cell_count, pointwise, depth_three, depth_five, classifier):
    weights = (pointwise.astype(jnp.float32).reshape(N_SEGMENT, SLOTS, 2, F, F), depth_three.astype(jnp.float32).reshape(N_SEGMENT, SLOTS, 9, F), depth_five.astype(jnp.float32).reshape(N_SEGMENT, SLOTS, 25, F))

    def image_loss(params, image, label):
        pair = jnp.stack([image, image])
        for section in range(N_SEGMENT):
            pair = segment_run(pair, params[0][section], params[1][section], params[2][section], cell_count[section])
        return head_loss(pair[1], classifier, label)
    grad_fn = jax.grad(image_loss)

    def device_sum(total, index):
        start = (index * MICRO).astype(jnp.int32)
        images = lax.dynamic_slice_in_dim(stem, start, MICRO, 0)
        marks = lax.dynamic_slice_in_dim(labels, start, MICRO, 0)
        partial_value = jax.tree.map(jnp.zeros_like, weights)
        for micro in range(MICRO):
            grads = grad_fn(weights, images[micro], marks[micro])
            partial_value = jax.tree.map(lambda a, b: a + b, partial_value, grads)
        rounded = jax.tree.map(lambda a: lax.optimization_barrier(a.astype(jnp.bfloat16)).astype(jnp.float32), partial_value)
        return (jax.tree.map(lambda a, b: a + b, total, rounded), None)
    start_total = jax.tree.map(jnp.zeros_like, weights)
    total, _ = lax.scan(device_sum, start_total, jnp.arange(N_DP, dtype=jnp.int32))
    return (total[0].reshape(CELLS, 2, F, F), total[1].reshape(CELLS, 9, F), total[2].reshape(CELLS, 25, F))
```

```python
import functools

import jax
import jax.numpy as jnp
from jax import lax
from jax.experimental import pallas as pl
from jax.experimental.pallas import tpu as pltpu
from jax.sharding import PartitionSpec as P

LOSS_SCALE = 256.0
SUB = 8
LANE = 128
BF = jnp.bfloat16
F32 = jnp.float32


class Dims:
    def __init__(self, images, side, feat):
        self.n = images
        self.side = side
        self.feat = feat
        self.parts = SUB // images
        self.tiles = feat // (self.parts * LANE)
        self.pos = side * side
        self.pad = -(-self.pos // SUB) * SUB
        self.rows = self.pos * SUB
        self.rows_pad = self.pad * SUB
        self.flat = images * self.pad

    def lanes(self, part, tile):
        start = (part * self.tiles + tile) * LANE
        return slice(start, start + LANE)


def valid_taps(side, width, y, x, sign):
    reach = width // 2
    found = []
    for row in range(width):
        for column in range(width):
            yy = y + sign * (row - reach)
            xx = x + sign * (column - reach)
            if 0 <= yy < side and 0 <= xx < side:
                found.append((row * width + column, yy * side + xx))
    return found


def spread_taps(d, source, slot, taps_ref):
    for tap in range(source.shape[0]):
        value = source[tap, slot : slot + 1]
        for part in range(d.parts):
            for tile in range(d.tiles):
                start = tap * SUB + part * d.n
                taps_ref[tile, start : start + d.n, :] = jnp.broadcast_to(
                    value[:, d.lanes(part, tile)], (d.n, LANE)
                )


def conv(d, x_ref, taps_ref, width, sign, emit):
    first = 0 if width == 3 else 9
    for tile in range(d.tiles):
        for y in range(d.side):
            for x in range(d.side):
                total = None
                for tap, at in valid_taps(d.side, width, y, x, sign):
                    w = taps_ref[tile, (first + tap) * SUB : (first + tap + 1) * SUB, :]
                    v = x_ref[tile, at * SUB : (at + 1) * SUB, :] * w
                    total = v if total is None else total + v
                emit(tile, y * d.side + x, total)


def to_rows(d, ref):
    images = []
    for image in range(d.n):
        pieces = []
        for part in range(d.parts):
            for tile in range(d.tiles):
                pieces.append(ref[tile, pl.ds(part * d.n + image, d.pad, stride=SUB), :])
        images.append(jnp.concatenate(pieces, axis=1))
    return jnp.concatenate(images, axis=0) if d.n > 1 else images[0]


def from_rows(d, value, ref):
    for image in range(d.n):
        for part in range(d.parts):
            for tile in range(d.tiles):
                ref[tile, pl.ds(part * d.n + image, d.pad, stride=SUB), :] = value[
                    image * d.pad : (image + 1) * d.pad, d.lanes(part, tile)
                ]


def at(position):
    return slice(position * SUB, (position + 1) * SUB)


def clear_tail(d, ref):
    ref[:, d.rows :, :] = jnp.zeros((d.tiles, d.rows_pad - d.rows, LANE), F32)


def branch_rows(d, value, width, taps, xs, cs):
    xs[...] = jnp.maximum(value.astype(F32), 0.0)

    def emit(tile, position, v):
        cs[tile, at(position), :] = v

    conv(d, xs, taps, width, 1, emit)
    return to_rows(d, cs).astype(BF)


def forward_cell(d, older, newer, slot, w, table, scr):
    taps, xs, cs = scr["taps"], scr["xs"], scr["cs"]
    spread_taps(d, table, slot, taps)
    rows_three = branch_rows(d, newer, 3, taps, xs, cs)
    rows_five = branch_rows(d, older, 5, taps, xs, cs)
    total = jnp.dot(rows_three, w[slot, 0], preferred_element_type=F32)
    total = total + jnp.dot(rows_five, w[slot, 1], preferred_element_type=F32)
    from_rows(d, total, cs)
    return cs[:, : d.rows, :].astype(BF)


def forward_section(d, count, w, table, res, last, scr):
    first = forward_cell(d, res[0], res[1], 0, w, table, scr)
    res[2] = first

    @pl.when(count > 1)
    def _():
        last[...] = forward_cell(d, res[1], res[2], 1, w, table, scr)

    @pl.when(count <= 1)
    def _():
        last[...] = res[2]


def slope(value):
    value = value.astype(F32)
    return jnp.where(value > 0, 1.0, jnp.where(value == 0, 0.5, 0.0))


def rounded(value):
    return value.astype(BF).astype(F32)


NT = (((1,), (1,)), ((), ()))
TN = (((0,), (0,)), ((), ()))


def backward_cell(d, slot, older, newer, w, table, scr, keep, cot, add_newer, out_newer, out_older, through=True):
    taps, xs, cs = scr["taps"], scr["xs"], scr["cs"]
    if through:
        spread_taps(d, table, slot, taps)
    rows = to_rows(d, cs).astype(BF)
    keep(slot, rows)
    for branch, width in ((0, 3), (1, 5)):
        back = lax.dot_general(rows, w[slot, branch], NT, preferred_element_type=F32)
        from_rows(d, rounded(back), cs)
        cot[2 * slot + branch] = cs[:, : d.rows, :].astype(BF)
        if not through:
            continue
        if branch == 0:

            def emit(tile, position, v):
                s = slope(newer[tile, at(position), :])
                xs[tile, at(position), :] = rounded(v) * s

            conv(d, cs, taps, 3, -1, emit)
            out_newer[...] = rounded(add_newer() + xs[...])
        else:

            def emit(tile, position, v):
                s = slope(older[tile, at(position), :])
                out_older[tile, at(position), :] = rounded(v) * s

            conv(d, cs, taps, 5, -1, emit)


def backward_section(d, info, w, table, res, blocks, cot, scr, out):
    cs, g0, g1, g2 = scr["cs"], scr["g0"], scr["g1"], scr["g2"]
    clear_tail(d, cs)
    count, place = info[1], info[2]
    depth, _, share = blocks.shape

    def keep(slot, rows):
        for other in range(depth):
            blocks[place ^ other, slot * d.flat : (slot + 1) * d.flat, :] = rows[
                :, other * share : (other + 1) * share
            ]

    @pl.when(count > 1)
    def _():
        cs[:, : d.rows, :] = g1[...]
        backward_cell(
            d, 1, res.at[1], res.at[2], w, table, scr, keep, cot, lambda: g0[...], g1, g2
        )

    @pl.when(count <= 1)
    def _():
        g2[...] = g0[...]
        blocks[:, d.flat : 2 * d.flat, :] = jnp.zeros((depth, d.flat, share), BF)
        cot[2] = jnp.zeros(cot.shape[1:], BF)
        cot[3] = jnp.zeros(cot.shape[1:], BF)

    cs[:, : d.rows, :] = g1[...]
    backward_cell(
        d, 0, res.at[0], res.at[1], w, table, scr, keep, cot, lambda: g2[...], g1, g0,
        through=out is not None,
    )
    if out is not None:
        out[0] = g0[...].astype(BF)
        out[1] = g1[...].astype(BF)


def head(d, final, label_ref, offset, classifier_ref, scr):
    g0, g1, hs = scr["g0"], scr["g1"], scr["hs"]
    for tile in range(d.tiles):
        total = None
        for position in range(d.pos):
            v = final[tile, at(position), :].astype(F32)
            total = v if total is None else total + v
        hs[tile] = total * (1.0 / d.pos)
    pieces = []
    for part in range(d.parts):
        for tile in range(d.tiles):
            pieces.append(hs[tile, part * d.n : (part + 1) * d.n, :])
    pooled = jnp.concatenate(pieces, axis=1)
    pooled = jnp.concatenate([pooled, jnp.zeros((SUB - d.n, d.feat), F32)], axis=0)

    def split(v):
        high = rounded(v)
        mid = rounded(v - high)
        low = v - high - mid
        return jnp.concatenate([high, mid, low, jnp.zeros_like(v)], axis=0).astype(BF)

    def joined(v):
        return v[0:SUB] + v[SUB : 2 * SUB] + v[2 * SUB : 3 * SUB]

    logits = joined(
        lax.dot_general(split(pooled), classifier_ref[...], NT, preferred_element_type=F32)
    )
    row = lax.broadcasted_iota(jnp.int32, logits.shape, 0)
    column = lax.broadcasted_iota(jnp.int32, logits.shape, 1)
    wanted = jnp.full(logits.shape, -1, jnp.int32)
    for image in range(d.n):
        wanted = jnp.where(row == image, label_ref[offset + image], wanted)
    target = jnp.where(column == wanted, 1.0, 0.0)
    back = LOSS_SCALE * (logits - target)
    pooled_cot = joined(
        jnp.dot(split(back), classifier_ref[...], preferred_element_type=F32)
    )
    each = rounded(pooled_cot * (1.0 / d.pos))
    for part in range(d.parts):
        for tile in range(d.tiles):
            hs[tile, part * d.n : (part + 1) * d.n, :] = each[: d.n, d.lanes(part, tile)]
    for tile in range(d.tiles):
        value = hs[tile]
        for position in range(d.pos):
            g1[tile, at(position), :] = value
    g0[...] = jnp.zeros(g0.shape, F32)


def load_stem(d, stem, chunk, cs):
    for y in range(d.side):
        for x in range(d.side):
            value = stem[y, x, chunk * d.n : (chunk + 1) * d.n]
            for part in range(d.parts):
                for tile in range(d.tiles):
                    start = (y * d.side + x) * SUB + part * d.n
                    cs[tile, start : start + d.n, :] = value[:, d.lanes(part, tile)]


SCRATCH = ("taps", "xs", "cs", "g0", "g1", "g2", "hs")


def scratch_shapes(d, n_taps):
    packed = (d.tiles, d.rows, LANE)
    return [
        pltpu.VMEM((d.tiles, n_taps * SUB, LANE), F32),
        pltpu.VMEM(packed, F32),
        pltpu.VMEM((d.tiles, d.rows_pad, LANE), F32),
        pltpu.VMEM(packed, F32),
        pltpu.VMEM(packed, F32),
        pltpu.VMEM(packed, F32),
        pltpu.VMEM((d.tiles, SUB, LANE), F32),
    ]


def hand_on(count, res, out):
    @pl.when(count > 1)
    def _():
        out[0] = res[2]

    @pl.when(count <= 1)
    def _():
        out[0] = res[1]


def take_stem(d, chunk, stem, res, scr):
    load_stem(d, stem, chunk, scr["cs"])
    value = scr["cs"][:, : d.rows, :].astype(BF)
    res[0] = value
    res[1] = value


def forward_kernel(d, chunk, step, info, pair, w, table, own_in, out, res, own, *rest):
    sems, scr = rest[-1], dict(zip(SCRATCH, rest))

    @pl.when(info[0] == step[0])
    def _():
        count = info[1]
        clear_tail(d, scr["cs"])
        if own_in is None:
            take_stem(d, chunk, pair, res, scr)
        else:
            res[0] = pair[0]
            res[1] = pair[1]
        copy = pltpu.make_async_copy(res.at[pl.ds(0, 2)], own, sems.at[0])
        copy.start()
        forward_section(d, count, w, table, res, out.at[1], scr)
        hand_on(count, res, out)
        copy.wait()


def fresh_kernel(d, chunk, step, info, stem, w, table, *rest):
    forward_kernel(d, chunk, step, info, stem, w, table, None, *rest)


def backward_kernel(d, step, info, cotangent, w, table, res, blocks_in, cot_in, out, blocks, cot, *rest):
    scr = dict(zip(SCRATCH, rest))

    @pl.when(info[0] == step[0])
    def _():
        scr["g0"][...] = cotangent[0].astype(F32)
        scr["g1"][...] = cotangent[1].astype(F32)
        backward_section(d, info, w, table, res, blocks, cot, scr, out)

    @pl.when(info[0] != step[0])
    def _():
        blocks[...] = blocks_in[...]
        cot[...] = cot_in[...]


def turn_kernel(d, chunk, step, info, labels, pair, w, table, classifier_in, own_in, out, res, own, blocks, cot, *rest):
    scr, (classifier, sems) = dict(zip(SCRATCH, rest)), rest[-2:]

    @pl.when(info[0] == step[0])
    def _():
        fetch = pltpu.make_async_copy(classifier_in, classifier, sems.at[1])
        fetch.start()
        clear_tail(d, scr["cs"])
        res[0] = pair[0]
        res[1] = pair[1]
        copy = pltpu.make_async_copy(res.at[pl.ds(0, 2)], own, sems.at[0])
        copy.start()
        forward_section(d, info[1], w, table, res, out.at[1], scr)
        fetch.wait()
        head(d, out.at[1], labels, chunk * d.n, classifier, scr)
        backward_section(d, info, w, table, res, blocks, cot, scr, out)
        copy.wait()


def send_kernel(d, n_chunks, n_taps, n_steps, depth, info, *refs):
    blocks, refs = refs[:n_chunks], refs[n_chunks:]
    every, cot = refs[: n_chunks * n_steps], refs[n_chunks * n_steps : n_chunks * (n_steps + 1)]
    refs = refs[n_chunks * (n_steps + 1) :]
    outs, (res, tap_blocks, xs, cs, sums) = refs[:depth], refs[depth:]
    slots = 2
    share = outs[0].shape[1]
    place = info[2]
    below = n_chunks * slots * d.flat
    for k in range(depth):
        for chunk in range(n_chunks):
            start = chunk * slots * d.flat
            outs[k][start : start + slots * d.flat, :] = blocks[chunk][k]
    for step in range(n_steps):

        @pl.when(info[0] == step)
        def _():
            for chunk in range(n_chunks):
                res[chunk] = every[chunk * n_steps + step][...]

    for slot in range(slots):
        for branch, width in ((0, 3), (1, 5)):
            first = slot * n_taps + (0 if width == 3 else 9)
            reach = width // 2
            for chunk in range(n_chunks):
                source = res[chunk][slot + 1 - branch]
                xs[...] = jnp.maximum(source.astype(F32), 0.0)
                cs[...] = cot[chunk][2 * slot + branch].astype(F32)
                for tile in range(d.tiles):
                    for row in range(width):
                        for column in range(width):
                            total = None
                            for y in range(d.side):
                                for x in range(d.side):
                                    yy, xx = y + row - reach, x + column - reach
                                    if 0 <= yy < d.side and 0 <= xx < d.side:
                                        v = (
                                            xs[tile, at(yy * d.side + xx), :]
                                            * cs[tile, at(y * d.side + x), :]
                                        )
                                        total = v if total is None else total + v
                            tap = first + row * width + column
                            if chunk == 0:
                                sums[tile, at(tap), :] = total
                            else:
                                sums[tile, at(tap), :] += total
    count = slots * n_taps
    padded = tap_blocks.shape[1]
    sums[:, count * SUB :, :] = jnp.zeros((d.tiles, (padded - count) * SUB, LANE), F32)
    pieces = []
    for part in range(d.parts):
        for tile in range(d.tiles):
            total = None
            for image in range(d.n):
                v = sums[tile, pl.ds(part * d.n + image, padded, stride=SUB), :]
                total = v if total is None else total + v
            pieces.append(total)
    value = jnp.concatenate(pieces, axis=1).astype(BF)
    for other in range(depth):
        tap_blocks[place ^ other] = value[:, other * share : (other + 1) * share]
    for k in range(depth):
        outs[k][below:, :] = tap_blocks[k]


def again_kernel(d, depth, n_chunks, info, w, table, *refs):
    lots = depth * n_chunks
    pairs, (acts, maps, fresh, taps, more, xs, cs, sems) = refs[:lots], refs[lots:]
    copies = [
        pltpu.make_async_copy(pairs[lot], maps.at[lot], sems.at[lot]) for lot in range(lots)
    ]
    for copy in copies:
        copy.start()
    clear_tail(d, cs)
    spread_taps(d, table, 0, taps)
    spread_taps(d, table, 1, more)
    for copy in copies:
        copy.wait()

    def place(lot):
        return pl.ds(pl.multiple_of(lot * d.flat, 16), d.flat)

    @pl.loop(0, lots)
    def _(lot):
        acts[0, place(lot), :] = branch_rows(d, maps[lot, 1], 3, taps, xs, cs)
        acts[1, place(lot), :] = branch_rows(d, maps[lot, 0], 5, taps, xs, cs)

    @pl.when(info[1] > 1)
    def _():
        fresh[...] = jnp.dot(acts[0], w[0, 0], preferred_element_type=F32)
        fresh[...] += jnp.dot(acts[1], w[0, 1], preferred_element_type=F32)

        @pl.loop(0, lots)
        def _(lot):
            acts[3, place(lot), :] = branch_rows(d, maps[lot, 1], 5, more, xs, cs)
            from_rows(d, fresh[place(lot), :], cs)
            value = cs[:, : d.rows, :].astype(BF)
            clear_tail(d, cs)
            acts[2, place(lot), :] = branch_rows(d, value, 3, more, xs, cs)

    @pl.when(info[1] <= 1)
    def _():
        acts[2:4] = jnp.zeros((2,) + acts.shape[1:], BF)


def product_kernel(d, n_chunks, depth, core, *refs):
    acts, blocks, (mine, other) = refs[0], refs[1:-2], refs[-2:]
    share = blocks[0].shape[-1]
    half = share // 2
    below = n_chunks * 2 * d.flat

    def write(low):
        high = half - low
        for slot in range(2):
            dh = [
                blocks[line][(2 * chunk + slot) * d.flat : (2 * chunk + slot + 1) * d.flat, :]
                for line in range(depth)
                for chunk in range(n_chunks)
            ]
            dh = jnp.concatenate(dh, axis=0)
            for branch in range(2):
                grad = lax.dot_general(
                    dh, acts[2 * slot + branch], TN, preferred_element_type=F32
                )
                rows = slice((2 * slot + branch) * half, (2 * slot + branch + 1) * half)
                mine[rows, :] = grad[low : low + half, :]
                other[rows, :] = grad[high : high + half, :].astype(BF)
        total = None
        for line in range(depth):
            v = blocks[line][below:, :].astype(F32)
            total = v if total is None else total + v
        mine[4 * half :, :half] = total[:, low : low + half]
        other[4 * half :, :] = jnp.concatenate(
            [total[:, high : high + half], jnp.zeros((total.shape[0], d.feat - half), F32)], axis=1
        ).astype(BF)

    @pl.when(core[0] == 0)
    def _():
        write(0)

    @pl.when(core[0] != 0)
    def _():
        write(half)


def sum_kernel(d, mine, received, grad, three, five):
    half = grad.shape[2]
    for slot in range(2):
        for branch in range(2):
            rows = slice((2 * slot + branch) * half, (2 * slot + branch + 1) * half)
            grad[slot, branch] = mine[rows, :] + received[rows, :].astype(F32)
    taps = mine[4 * half :, :half] + received[4 * half :, :].astype(F32)[:, :half]
    n_three, n_five = three.shape[0], five.shape[0]
    for slot in range(2):
        first = slot * (n_three + n_five)
        for tap in range(n_three):
            three[tap, slot : slot + 1, :] = taps[first + tap : first + tap + 1, :]
        for tap in range(n_five):
            row = first + n_three + tap
            five[tap, slot : slot + 1, :] = taps[row : row + 1, :]


VM = pl.BlockSpec(memory_space=pltpu.VMEM)
SM = pl.BlockSpec(memory_space=pltpu.SMEM)
ANY = pl.BlockSpec(memory_space=pl.ANY)
PARAMS = pltpu.CompilerParams(vmem_limit_bytes=12 * 1024 * 1024)
SHORT = pl.CostEstimate(flops=10**6, bytes_accessed=10**4, transcendentals=0)
WIDE = pltpu.CompilerParams(vmem_limit_bytes=20 * 1024 * 1024)


def exchange(value, axis, pairs):
    return lax.ppermute(value, axis, pairs)


def neighbour_pairs(size, low):
    if size == 1:
        return [(0, 0)]
    if low % 2 == 0:
        return [(i, i ^ 1) if (i ^ 1) < size else (i, i) for i in range(size)]
    return [(i, (i + 1) % size if i % 2 else (i - 1) % size) for i in range(size)]


CHUNKS = 2


def per_device(stem, labels, cell_count, pointwise, depth_three, depth_five, classifier):
    segments = lax.axis_size("segment")
    replicas = lax.axis_size("dp")
    here = lax.axis_index("segment").astype(jnp.int32)
    replica = lax.axis_index("dp").astype(jnp.int32)
    depth = replicas // 2
    info = jnp.stack([here, cell_count[0], replica // 2])
    core = (replica % 2).reshape(1)
    micro, side, _, feat = stem.shape
    slots = pointwise.shape[0]
    d = Dims(micro // CHUNKS, side, feat)
    n_three, n_five = depth_three.shape[1], depth_five.shape[1]
    n_taps = n_three + n_five
    share = feat // depth
    half = share // 2
    packed = (d.tiles, d.rows, LANE)
    pair_t = jax.ShapeDtypeStruct((2,) + packed, BF)
    res_t = jax.ShapeDtypeStruct((3,) + packed, BF)
    cot_t = jax.ShapeDtypeStruct((4,) + packed, BF)
    blocks_t = jax.ShapeDtypeStruct((depth, slots * d.flat, share), BF)
    scratch = scratch_shapes(d, n_taps)
    stem_t = stem.transpose(1, 2, 0, 3).astype(F32)
    table = jnp.concatenate([depth_three.transpose(1, 0, 2), depth_five.transpose(1, 0, 2)], axis=0)
    weights = (pointwise, table.astype(F32))

    def at_step(step):
        return jnp.full((1,), step, jnp.int32)

    def forward_call(chunk, fresh):
        return jax.jit(
            pl.pallas_call(
                functools.partial(fresh_kernel if fresh else forward_kernel, d, chunk),
                out_shape=(pair_t, res_t, pair_t),
                in_specs=[SM, SM, VM, VM, VM] + [ANY] * (0 if fresh else 1),
                out_specs=(VM, VM, ANY),
                scratch_shapes=scratch + [pltpu.SemaphoreType.DMA((1,))],
                input_output_aliases={} if fresh else {5: 2},
                compiler_params=PARAMS,
                cost_estimate=SHORT,
                name="forward",
            )
        )

    def turn_call(chunk):
        return jax.jit(
            pl.pallas_call(
                functools.partial(turn_kernel, d, chunk),
                out_shape=(pair_t, res_t, pair_t, blocks_t, cot_t),
                in_specs=[SM, SM, SM, VM, VM, VM, ANY, ANY],
                out_specs=(VM, VM, ANY, VM, VM),
                scratch_shapes=scratch
                + [pltpu.VMEM(classifier.shape[::-1], BF), pltpu.SemaphoreType.DMA((2,))],
                input_output_aliases={7: 2},
                compiler_params=PARAMS,
                cost_estimate=SHORT,
                name="turn",
            )
        )

    def backward_body(has_out):
        def body(step, info, g, w, table, res, blocks_in, cot_in, *rest):
            out, rest = (rest[0], rest[1:]) if has_out else (None, rest)
            backward_kernel(d, step, info, g, w, table, res, blocks_in, cot_in, out, *rest)

        return body

    def backward_call(has_out):
        first = 1 if has_out else 0
        return jax.jit(
            pl.pallas_call(
                backward_body(has_out),
                out_shape=((pair_t,) if has_out else ()) + (blocks_t, cot_t),
                in_specs=[SM, SM] + [VM] * 6,
                out_specs=(VM,) * (2 + first),
                scratch_shapes=scratch,
                input_output_aliases={6: first, 7: first + 1},
                compiler_params=PARAMS,
                cost_estimate=SHORT,
                name="backward",
            )
        )

    res = [[] for _ in range(CHUNKS)]
    owns = [None] * CHUNKS
    moving = [None] * CHUNKS
    blocks = [None] * CHUNKS
    cot = [None] * CHUNKS

    forward = forward_call(None, False)
    for step in range(segments - 1):
        for c in range(CHUNKS):
            if step > 0:
                args = (at_step(step), info, moving[c], *weights, owns[c])
                out, kept, owns[c] = forward(*args)
            else:
                args = (at_step(step), info, stem_t, *weights)
                out, kept, owns[c] = forward_call(c, True)(*args)
            res[c].append(kept)
            moving[c] = exchange(out, "segment", neighbour_pairs(segments, step))
    for c in range(CHUNKS):
        out, kept, owns[c], blocks[c], cot[c] = turn_call(c)(
            at_step(segments - 1), info, labels, moving[c], *weights, classifier.T, owns[c]
        )
        res[c].append(kept)
        moving[c] = exchange(out, "segment", neighbour_pairs(segments, segments - 2))

    def along_line(value, k):
        return exchange(value, "dp", [(i, i ^ (2 * k)) for i in range(replicas)])

    gathered = []
    for c in range(CHUNKS):
        own = owns[c]
        if gathered:
            own, gathered[-1] = lax.optimization_barrier((own, gathered[-1]))
        gathered.append([own] + [along_line(own, k) for k in range(1, depth)])

    backward, backward_end = backward_call(True), backward_call(False)
    for step in range(segments - 2, -1, -1):
        for c in range(CHUNKS):
            args = (at_step(step), info, moving[c], *weights, res[c][step], blocks[c], cot[c])
            if step > 0:
                out, blocks[c], cot[c] = backward(*args)
                moving[c] = exchange(out, "segment", neighbour_pairs(segments, step - 1))
            else:
                blocks[c], cot[c] = backward_end(*args)

    tap_rows = -(-slots * n_taps // 16) * 16
    total_rows = CHUNKS * slots * d.flat + tap_rows
    sent = pl.pallas_call(
        functools.partial(send_kernel, d, CHUNKS, n_taps, segments, depth),
        out_shape=(jax.ShapeDtypeStruct((total_rows, share), BF),) * depth,
        in_specs=[SM] + [VM] * (CHUNKS * (segments + 2)),
        out_specs=(VM,) * depth,
        scratch_shapes=[
            pltpu.VMEM((CHUNKS, 3) + packed, BF),
            pltpu.VMEM((depth, tap_rows, share), BF),
            pltpu.VMEM(packed, F32),
            pltpu.VMEM(packed, F32),
            pltpu.VMEM((d.tiles, tap_rows * SUB, LANE), F32),
        ],
        compiler_params=WIDE,
        cost_estimate=SHORT,
        name="send",
    )(info, *blocks, *[r for chunk in res for r in chunk], *cot)
    received = [sent[0]] + [along_line(sent[k], k) for k in range(1, depth)]

    lots = depth * CHUNKS
    acts = pl.pallas_call(
        functools.partial(again_kernel, d, depth, CHUNKS),
        out_shape=jax.ShapeDtypeStruct((4, lots * d.flat, feat), BF),
        in_specs=[SM] + [VM] * 2 + [ANY] * lots,
        out_specs=VM,
        scratch_shapes=[
            pltpu.VMEM((lots, 2) + packed, BF),
            pltpu.VMEM((lots * d.flat, feat), F32),
            scratch[0],
            scratch[0],
            scratch[1],
            scratch[2],
            pltpu.SemaphoreType.DMA((lots,)),
        ],
        compiler_params=WIDE,
        cost_estimate=SHORT,
        name="again",
    )(info, *weights, *[gathered[c][k] for k in range(depth) for c in range(CHUNKS)])
    sum_t = (4 * half + tap_rows, feat)
    mine, other = pl.pallas_call(
        functools.partial(product_kernel, d, CHUNKS, depth),
        out_shape=(jax.ShapeDtypeStruct(sum_t, F32), jax.ShapeDtypeStruct(sum_t, BF)),
        in_specs=[SM] + [VM] * (1 + depth),
        out_specs=(VM, VM),
        compiler_params=WIDE,
        cost_estimate=SHORT,
        name="product",
    )(core, acts, *received)
    swapped = exchange(other, "dp", [(i, i ^ 1) for i in range(replicas)])
    grad, three, five = pl.pallas_call(
        functools.partial(sum_kernel, d),
        out_shape=(
            jax.ShapeDtypeStruct((slots, 2, half, feat), F32),
            jax.ShapeDtypeStruct((n_three, slots, half), F32),
            jax.ShapeDtypeStruct((n_five, slots, half), F32),
        ),
        in_specs=[VM, VM],
        out_specs=(VM,) * 3,
        compiler_params=PARAMS,
        cost_estimate=SHORT,
        name="sum",
    )(mine, swapped)
    return (
        grad.transpose(0, 1, 3, 2),
        three.transpose(1, 0, 2),
        five.transpose(1, 0, 2),
    )


def solution(mesh):
    return jax.shard_map(
        per_device,
        mesh=mesh,
        in_specs=(
            P("dp", None, None, None),
            P("dp"),
            P("segment"),
            P("segment", None, None, None),
            P("segment", None, None),
            P("segment", None, None),
            P(),
        ),
        out_specs=(
            P("segment", None, None, "dp"),
            P("segment", None, "dp"),
            P("segment", None, "dp"),
        ),
        check_vma=False,
    )
```

```python
import functools

import jax
import jax.numpy as jnp
from jax import lax
from jax.experimental import pallas as pl
from jax.experimental.pallas import tpu as pltpu
from jax.sharding import PartitionSpec as P

LOSS_SCALE = 256.0
SUB = 8
LANE = 128
BF = jnp.bfloat16
F32 = jnp.float32


class Dims:
    def __init__(self, images, side, feat):
        self.n = images
        self.side = side
        self.feat = feat
        self.parts = SUB // images
        self.tiles = feat // (self.parts * LANE)
        self.pos = side * side
        self.pad = -(-self.pos // SUB) * SUB
        self.rows = self.pos * SUB
        self.rows_pad = self.pad * SUB
        self.flat = images * self.pad

    def lanes(self, part, tile):
        start = (part * self.tiles + tile) * LANE
        return slice(start, start + LANE)


def valid_taps(side, width, y, x, sign):
    reach = width // 2
    found = []
    for row in range(width):
        for column in range(width):
            yy = y + sign * (row - reach)
            xx = x + sign * (column - reach)
            if 0 <= yy < side and 0 <= xx < side:
                found.append((row * width + column, yy * side + xx))
    return found


def spread_taps(d, source, slot, taps_ref):
    for tap in range(source.shape[0] - d.pos):
        value = source[tap, slot : slot + 1]
        for part in range(d.parts):
            for tile in range(d.tiles):
                start = tap * SUB + part * d.n
                taps_ref[tile, start : start + d.n, :] = jnp.broadcast_to(
                    value[:, d.lanes(part, tile)], (d.n, LANE)
                )


def conv(d, x_ref, taps_ref, width, sign, emit):
    first = 0 if width == 3 else 9
    for tile in range(d.tiles):
        for y in range(d.side):
            for x in range(d.side):
                total = None
                for tap, at in valid_taps(d.side, width, y, x, sign):
                    w = taps_ref[tile, (first + tap) * SUB : (first + tap + 1) * SUB, :]
                    v = x_ref[tile, at * SUB : (at + 1) * SUB, :] * w
                    total = v if total is None else total + v
                emit(tile, y * d.side + x, total)


def to_rows(d, ref):
    images = []
    for image in range(d.n):
        pieces = []
        for part in range(d.parts):
            for tile in range(d.tiles):
                pieces.append(ref[tile, pl.ds(part * d.n + image, d.pad, stride=SUB), :])
        images.append(jnp.concatenate(pieces, axis=1))
    return jnp.concatenate(images, axis=0) if d.n > 1 else images[0]


def from_rows(d, value, ref):
    for image in range(d.n):
        for part in range(d.parts):
            for tile in range(d.tiles):
                ref[tile, pl.ds(part * d.n + image, d.pad, stride=SUB), :] = value[
                    image * d.pad : (image + 1) * d.pad, d.lanes(part, tile)
                ]


def at(position):
    return slice(position * SUB, (position + 1) * SUB)


def clear_tail(d, ref):
    ref[:, d.rows :, :] = jnp.zeros((d.tiles, d.rows_pad - d.rows, LANE), F32)


def branch_rows(d, value, width, taps, xs, cs):
    xs[...] = jnp.maximum(value.astype(F32), 0.0)

    def emit(tile, position, v):
        cs[tile, at(position), :] = v

    conv(d, xs, taps, width, 1, emit)
    return to_rows(d, cs).astype(BF)


def forward_cell(d, older, newer, slot, w, table, scr):
    taps, xs, cs = scr["taps"], scr["xs"], scr["cs"]
    spread_taps(d, table, slot, taps)
    rows_three = branch_rows(d, newer, 3, taps, xs, cs)
    rows_five = branch_rows(d, older, 5, taps, xs, cs)
    total = jnp.dot(rows_three, w[slot, 0], preferred_element_type=F32)
    total = total + jnp.dot(rows_five, w[slot, 1], preferred_element_type=F32)
    from_rows(d, total, cs)
    return cs[:, : d.rows, :].astype(BF)


def forward_section(d, count, w, table, res, last, scr):
    first = forward_cell(d, res[0], res[1], 0, w, table, scr)
    res[2] = first

    @pl.when(count > 1)
    def _():
        last[...] = forward_cell(d, res[1], res[2], 1, w, table, scr)

    @pl.when(count <= 1)
    def _():
        last[...] = res[2]


def slope(value):
    value = value.astype(F32)
    return jnp.where(value > 0, 1.0, jnp.where(value == 0, 0.5, 0.0))


def rounded(value):
    return value.astype(BF).astype(F32)


NT = (((1,), (1,)), ((), ()))
TN = (((0,), (0,)), ((), ()))


def backward_cell(d, slot, older, newer, w, table, scr, keep, cot, add_newer, out_newer, out_older, through=True):
    taps, xs, cs = scr["taps"], scr["xs"], scr["cs"]
    if through:
        spread_taps(d, table, slot, taps)
    rows = to_rows(d, cs).astype(BF)
    keep(slot, rows)
    for branch, width in ((0, 3), (1, 5)):
        back = lax.dot_general(rows, w[slot, branch], NT, preferred_element_type=F32)
        from_rows(d, rounded(back), cs)
        cot[2 * slot + branch] = cs[:, : d.rows, :].astype(BF)
        if not through:
            continue
        if branch == 0:

            def emit(tile, position, v):
                s = slope(newer[tile, at(position), :])
                xs[tile, at(position), :] = rounded(v) * s

            conv(d, cs, taps, 3, -1, emit)
            out_newer[...] = rounded(add_newer() + xs[...])
        else:

            def emit(tile, position, v):
                s = slope(older[tile, at(position), :])
                out_older[tile, at(position), :] = rounded(v) * s

            conv(d, cs, taps, 5, -1, emit)


def backward_section(d, info, w, table, res, blocks, cot, scr, out):
    cs, g0, g1, g2 = scr["cs"], scr["g0"], scr["g1"], scr["g2"]
    clear_tail(d, cs)
    count, place = info[1], info[2]
    depth, _, share = blocks.shape

    def keep(slot, rows):
        for other in range(depth):
            blocks[place ^ other, slot * d.flat : (slot + 1) * d.flat, :] = rows[
                :, other * share : (other + 1) * share
            ]

    @pl.when(count > 1)
    def _():
        cs[:, : d.rows, :] = g1[...]
        backward_cell(
            d, 1, res.at[1], res.at[2], w, table, scr, keep, cot, lambda: g0[...], g1, g2
        )

    @pl.when(count <= 1)
    def _():
        g2[...] = g0[...]
        blocks[:, d.flat : 2 * d.flat, :] = jnp.zeros((depth, d.flat, share), BF)
        cot[2] = jnp.zeros(cot.shape[1:], BF)
        cot[3] = jnp.zeros(cot.shape[1:], BF)

    cs[:, : d.rows, :] = g1[...]
    backward_cell(
        d, 0, res.at[0], res.at[1], w, table, scr, keep, cot, lambda: g2[...], g1, g0,
        through=out is not None,
    )
    if out is not None:
        out[0] = g0[...].astype(BF)
        out[1] = g1[...].astype(BF)


def head(d, final, label_ref, offset, classifier_ref, scr):
    g0, g1, hs = scr["g0"], scr["g1"], scr["hs"]
    for tile in range(d.tiles):
        total = None
        for position in range(d.pos):
            v = final[tile, at(position), :].astype(F32)
            total = v if total is None else total + v
        hs[tile] = total * (1.0 / d.pos)
    pieces = []
    for part in range(d.parts):
        for tile in range(d.tiles):
            pieces.append(hs[tile, part * d.n : (part + 1) * d.n, :])
    pooled = jnp.concatenate(pieces, axis=1)
    pooled = jnp.concatenate([pooled, jnp.zeros((SUB - d.n, d.feat), F32)], axis=0)

    def split(v):
        high = rounded(v)
        mid = rounded(v - high)
        low = v - high - mid
        return jnp.concatenate([high, mid, low, jnp.zeros_like(v)], axis=0).astype(BF)

    def joined(v):
        return v[0:SUB] + v[SUB : 2 * SUB] + v[2 * SUB : 3 * SUB]

    logits = joined(
        lax.dot_general(split(pooled), classifier_ref[...], NT, preferred_element_type=F32)
    )
    row = lax.broadcasted_iota(jnp.int32, logits.shape, 0)
    column = lax.broadcasted_iota(jnp.int32, logits.shape, 1)
    wanted = jnp.full(logits.shape, -1, jnp.int32)
    for image in range(d.n):
        wanted = jnp.where(row == image, label_ref[offset + image], wanted)
    target = jnp.where(column == wanted, 1.0, 0.0)
    back = LOSS_SCALE * (logits - target)
    pooled_cot = joined(
        jnp.dot(split(back), classifier_ref[...], preferred_element_type=F32)
    )
    each = rounded(pooled_cot * (1.0 / d.pos))
    for part in range(d.parts):
        for tile in range(d.tiles):
            hs[tile, part * d.n : (part + 1) * d.n, :] = each[: d.n, d.lanes(part, tile)]
    for tile in range(d.tiles):
        value = hs[tile]
        for position in range(d.pos):
            g1[tile, at(position), :] = value
    g0[...] = jnp.zeros(g0.shape, F32)


def load_stem(d, n_taps, chunk, table, cs):
    for position in range(d.pos):
        value = table[n_taps + position, chunk * d.n : (chunk + 1) * d.n]
        for part in range(d.parts):
            for tile in range(d.tiles):
                start = position * SUB + part * d.n
                cs[tile, start : start + d.n, :] = value[:, d.lanes(part, tile)]


SCRATCH = ("taps", "xs", "cs", "g0", "g1", "g2", "hs")


def scratch_shapes(d, n_taps):
    packed = (d.tiles, d.rows, LANE)
    return [
        pltpu.VMEM((d.tiles, n_taps * SUB, LANE), F32),
        pltpu.VMEM(packed, F32),
        pltpu.VMEM((d.tiles, d.rows_pad, LANE), F32),
        pltpu.VMEM(packed, F32),
        pltpu.VMEM(packed, F32),
        pltpu.VMEM(packed, F32),
        pltpu.VMEM((d.tiles, SUB, LANE), F32),
    ]


def hand_on(count, res, out):
    @pl.when(count > 1)
    def _():
        out[0] = res[2]

    @pl.when(count <= 1)
    def _():
        out[0] = res[1]


def take_stem(d, chunk, table, res, scr):
    load_stem(d, table.shape[0] - d.pos, chunk, table, scr["cs"])
    value = scr["cs"][:, : d.rows, :].astype(BF)
    res[0] = value
    res[1] = value


def forward_kernel(d, chunk, fresh, step, info, pair, w, table, own_in, out, res, own, *rest):
    sems, scr = rest[-1], dict(zip(SCRATCH, rest))

    @pl.when(info[0] == step[0])
    def _():
        count = info[1]
        clear_tail(d, scr["cs"])
        if fresh:
            take_stem(d, chunk, table, res, scr)
        else:
            res[0] = pair[0]
            res[1] = pair[1]
        copy = pltpu.make_async_copy(res.at[pl.ds(0, 2)], own.at[chunk], sems.at[0])
        copy.start()
        forward_section(d, count, w, table, res, out.at[1], scr)
        hand_on(count, res, out)
        copy.wait()


def fresh_kernel(d, chunk, step, info, w, table, *rest):
    passed = [None] if chunk == 0 else []
    forward_kernel(d, chunk, True, step, info, None, w, table, *passed, *rest)


def backward_kernel(d, step, info, cotangent, w, table, res, blocks_in, cot_in, out, blocks, cot, *rest):
    scr = dict(zip(SCRATCH, rest))

    @pl.when(info[0] == step[0])
    def _():
        scr["g0"][...] = cotangent[0].astype(F32)
        scr["g1"][...] = cotangent[1].astype(F32)
        backward_section(d, info, w, table, res, blocks, cot, scr, out)

    @pl.when(info[0] != step[0])
    def _():
        blocks[...] = blocks_in[...]
        cot[...] = cot_in[...]


def turn_kernel(d, chunk, step, info, labels, pair, w, table, classifier_in, own_in, out, res, own, blocks, cot, *rest):
    scr, (classifier, sems) = dict(zip(SCRATCH, rest)), rest[-2:]

    @pl.when(info[0] == step[0])
    def _():
        fetch = pltpu.make_async_copy(classifier_in, classifier, sems.at[1])
        fetch.start()
        clear_tail(d, scr["cs"])
        res[0] = pair[0]
        res[1] = pair[1]
        copy = pltpu.make_async_copy(res.at[pl.ds(0, 2)], own.at[chunk], sems.at[0])
        copy.start()
        forward_section(d, info[1], w, table, res, out.at[1], scr)
        fetch.wait()
        head(d, out.at[1], labels, chunk * d.n, classifier, scr)
        backward_section(d, info, w, table, res, blocks, cot, scr, out)
        copy.wait()


def send_kernel(d, n_chunks, n_taps, n_steps, depth, info, *refs):
    blocks, refs = refs[:n_chunks], refs[n_chunks:]
    every, cot = refs[: n_chunks * n_steps], refs[n_chunks * n_steps : n_chunks * (n_steps + 1)]
    refs = refs[n_chunks * (n_steps + 1) :]
    outs, (res, tap_blocks, xs, cs, sums) = refs[:depth], refs[depth:]
    slots = 2
    share = outs[0].shape[1]
    place = info[2]
    below = n_chunks * slots * d.flat
    for k in range(depth):
        for chunk in range(n_chunks):
            start = chunk * slots * d.flat
            outs[k][start : start + slots * d.flat, :] = blocks[chunk][k]
    for step in range(n_steps):

        @pl.when(info[0] == step)
        def _():
            for chunk in range(n_chunks):
                res[chunk] = every[chunk * n_steps + step][...]

    for slot in range(slots):
        for branch, width in ((0, 3), (1, 5)):
            first = slot * n_taps + (0 if width == 3 else 9)
            reach = width // 2
            for chunk in range(n_chunks):
                source = res[chunk][slot + 1 - branch]
                xs[...] = jnp.maximum(source.astype(F32), 0.0)
                cs[...] = cot[chunk][2 * slot + branch].astype(F32)
                for tile in range(d.tiles):
                    for row in range(width):
                        for column in range(width):
                            total = None
                            for y in range(d.side):
                                for x in range(d.side):
                                    yy, xx = y + row - reach, x + column - reach
                                    if 0 <= yy < d.side and 0 <= xx < d.side:
                                        v = (
                                            xs[tile, at(yy * d.side + xx), :]
                                            * cs[tile, at(y * d.side + x), :]
                                        )
                                        total = v if total is None else total + v
                            tap = first + row * width + column
                            if chunk == 0:
                                sums[tile, at(tap), :] = total
                            else:
                                sums[tile, at(tap), :] += total
    count = slots * n_taps
    padded = tap_blocks.shape[1]
    sums[:, count * SUB :, :] = jnp.zeros((d.tiles, (padded - count) * SUB, LANE), F32)
    pieces = []
    for part in range(d.parts):
        for tile in range(d.tiles):
            total = None
            for image in range(d.n):
                v = sums[tile, pl.ds(part * d.n + image, padded, stride=SUB), :]
                total = v if total is None else total + v
            pieces.append(total)
    value = jnp.concatenate(pieces, axis=1).astype(BF)
    for other in range(depth):
        tap_blocks[place ^ other] = value[:, other * share : (other + 1) * share]
    for k in range(depth):
        outs[k][below:, :] = tap_blocks[k]


def again_kernel(d, places, depth, n_chunks, counts, where, w, table, *refs):
    ends, middles, (acts, maps, fresh, taps, more, xs, cs, sems) = (
        refs[:depth], refs[depth : 2 * depth], refs[2 * depth :]
    )
    lots = depth * n_chunks

    def fetch(sources):
        return [
            pltpu.make_async_copy(
                sources[line], maps.at[pl.ds(line * n_chunks, n_chunks)], sems.at[line]
            )
            for line in range(depth)
        ]

    copies = fetch(ends)
    at_end = jnp.logical_or(where[0] == 0, where[0] == places - 1)

    @pl.when(at_end)
    def _():
        for copy in copies:
            copy.start()

    @pl.when(jnp.logical_not(at_end))
    def _():
        for copy in fetch(middles):
            copy.start()

    clear_tail(d, cs)
    spread_taps(d, table, 0, taps)
    spread_taps(d, table, 1, more)
    for copy in copies:
        copy.wait()

    def place(lot):
        return pl.ds(pl.multiple_of(lot * d.flat, 16), d.flat)

    @pl.loop(0, lots)
    def _(lot):
        acts[0, place(lot), :] = branch_rows(d, maps[lot, 1], 3, taps, xs, cs)
        acts[1, place(lot), :] = branch_rows(d, maps[lot, 0], 5, taps, xs, cs)

    @pl.when(counts[0] > 1)
    def _():
        fresh[...] = jnp.dot(acts[0], w[0, 0], preferred_element_type=F32)
        fresh[...] += jnp.dot(acts[1], w[0, 1], preferred_element_type=F32)

        @pl.loop(0, lots)
        def _(lot):
            acts[3, place(lot), :] = branch_rows(d, maps[lot, 1], 5, more, xs, cs)
            from_rows(d, fresh[place(lot), :], cs)
            value = cs[:, : d.rows, :].astype(BF)
            clear_tail(d, cs)
            acts[2, place(lot), :] = branch_rows(d, value, 3, more, xs, cs)

    @pl.when(counts[0] <= 1)
    def _():
        acts[2:4] = jnp.zeros((2,) + acts.shape[1:], BF)


def product_kernel(d, n_chunks, depth, n_acts, core, *refs):
    acts, blocks, (mine, other) = refs[:n_acts], refs[n_acts:-2], refs[-2:]
    each = depth // n_acts
    share = blocks[0].shape[-1]
    half = share // 2
    below = n_chunks * 2 * d.flat

    def write(low):
        high = half - low
        for slot in range(2):
            dh = []
            for group in range(n_acts):
                pieces = [
                    blocks[line][(2 * chunk + slot) * d.flat : (2 * chunk + slot + 1) * d.flat, :]
                    for line in range(group * each, (group + 1) * each)
                    for chunk in range(n_chunks)
                ]
                dh.append(jnp.concatenate(pieces, axis=0))
            for branch in range(2):
                grad = None
                for group in range(n_acts):
                    v = lax.dot_general(
                        dh[group], acts[group][2 * slot + branch], TN, preferred_element_type=F32
                    )
                    grad = v if grad is None else grad + v
                rows = slice((2 * slot + branch) * half, (2 * slot + branch + 1) * half)
                mine[rows, :] = grad[low : low + half, :]
                other[rows, :] = grad[high : high + half, :].astype(BF)
        total = None
        for line in range(depth):
            v = blocks[line][below:, :].astype(F32)
            total = v if total is None else total + v
        mine[4 * half :, :half] = total[:, low : low + half]
        other[4 * half :, :] = jnp.concatenate(
            [total[:, high : high + half], jnp.zeros((total.shape[0], d.feat - half), F32)], axis=1
        ).astype(BF)

    @pl.when(core[0] == 0)
    def _():
        write(0)

    @pl.when(core[0] != 0)
    def _():
        write(half)


def sum_kernel(d, mine, received, grad, three, five):
    half = grad.shape[2]
    for slot in range(2):
        for branch in range(2):
            rows = slice((2 * slot + branch) * half, (2 * slot + branch + 1) * half)
            grad[slot, branch] = mine[rows, :] + received[rows, :].astype(F32)
    taps = mine[4 * half :, :half] + received[4 * half :, :].astype(F32)[:, :half]
    n_three, n_five = three.shape[0], five.shape[0]
    for slot in range(2):
        first = slot * (n_three + n_five)
        for tap in range(n_three):
            three[tap, slot : slot + 1, :] = taps[first + tap : first + tap + 1, :]
        for tap in range(n_five):
            row = first + n_three + tap
            five[tap, slot : slot + 1, :] = taps[row : row + 1, :]


VM = pl.BlockSpec(memory_space=pltpu.VMEM)
SM = pl.BlockSpec(memory_space=pltpu.SMEM)
ANY = pl.BlockSpec(memory_space=pl.ANY)
PARAMS = pltpu.CompilerParams(vmem_limit_bytes=7 * 1024 * 1024)
SHORT = pl.CostEstimate(flops=10**6, bytes_accessed=10**4, transcendentals=0)
LONG_LINE = pltpu.CompilerParams(vmem_limit_bytes=40 * 1024 * 1024)
WIDE = pltpu.CompilerParams(vmem_limit_bytes=10 * 1024 * 1024)


def exchange(value, axis, pairs):
    return lax.ppermute(value, axis, pairs)


def neighbour_pairs(size, low):
    if size == 1:
        return [(0, 0)]
    if low % 2 == 0:
        return [(i, i ^ 1) if (i ^ 1) < size else (i, i) for i in range(size)]
    return [(i, (i + 1) % size if i % 2 else (i - 1) % size) for i in range(size)]


CHUNKS = 2


def per_device(stem, labels, cell_count, pointwise, depth_three, depth_five, classifier):
    segments = lax.axis_size("segment")
    replicas = lax.axis_size("dp")
    here = lax.axis_index("segment").astype(jnp.int32)
    replica = lax.axis_index("dp").astype(jnp.int32)
    depth = replicas // 2
    info = jnp.stack([here, cell_count[0], replica // 2])
    core = (replica % 2).reshape(1)
    micro, side, _, feat = stem.shape
    slots = pointwise.shape[0]
    d = Dims(micro // CHUNKS, side, feat)
    n_three, n_five = depth_three.shape[1], depth_five.shape[1]
    n_taps = n_three + n_five
    share = feat // depth
    half = share // 2
    packed = (d.tiles, d.rows, LANE)
    pair_t = jax.ShapeDtypeStruct((2,) + packed, BF)
    own_t = jax.ShapeDtypeStruct((CHUNKS, 2) + packed, BF)
    res_t = jax.ShapeDtypeStruct((3,) + packed, BF)
    cot_t = jax.ShapeDtypeStruct((4,) + packed, BF)
    blocks_t = jax.ShapeDtypeStruct((depth, slots * d.flat, share), BF)
    scratch = scratch_shapes(d, n_taps)
    wider = ((0, 0), (0, micro - slots), (0, 0))
    table = jnp.concatenate(
        [
            jnp.pad(depth_three.transpose(1, 0, 2), wider),
            jnp.pad(depth_five.transpose(1, 0, 2), wider),
            stem.transpose(1, 2, 0, 3).reshape(side * side, micro, feat),
        ],
        axis=0,
    ).astype(F32)
    weights = (pointwise, table)

    def at_step(step):
        return jnp.full((1,), step, jnp.int32)

    def forward_call(chunk, fresh):
        begin = fresh and chunk == 0
        body = (
            functools.partial(fresh_kernel, d, chunk)
            if fresh
            else functools.partial(forward_kernel, d, chunk, False)
        )
        own_at = 4 if fresh else 5
        return jax.jit(
            pl.pallas_call(
                body,
                out_shape=(pair_t, res_t, own_t),
                in_specs=[SM, SM] + [VM] * (own_at - 2) + [ANY] * (0 if begin else 1),
                out_specs=(VM, VM, ANY),
                scratch_shapes=scratch + [pltpu.SemaphoreType.DMA((1,))],
                input_output_aliases={} if begin else {own_at: 2},
                compiler_params=PARAMS,
                cost_estimate=SHORT,
                name="forward",
            )
        )

    def turn_call(chunk):
        return jax.jit(
            pl.pallas_call(
                functools.partial(turn_kernel, d, chunk),
                out_shape=(pair_t, res_t, own_t, blocks_t, cot_t),
                in_specs=[SM, SM, SM, VM, VM, VM, ANY, ANY],
                out_specs=(VM, VM, ANY, VM, VM),
                scratch_shapes=scratch
                + [pltpu.VMEM(classifier.shape[::-1], BF), pltpu.SemaphoreType.DMA((2,))],
                input_output_aliases={7: 2},
                compiler_params=PARAMS,
                cost_estimate=SHORT,
                name="turn",
            )
        )

    def backward_body(has_out):
        def body(step, info, g, w, table, res, blocks_in, cot_in, *rest):
            out, rest = (rest[0], rest[1:]) if has_out else (None, rest)
            backward_kernel(d, step, info, g, w, table, res, blocks_in, cot_in, out, *rest)

        return body

    def backward_call(has_out):
        first = 1 if has_out else 0
        return jax.jit(
            pl.pallas_call(
                backward_body(has_out),
                out_shape=((pair_t,) if has_out else ()) + (blocks_t, cot_t),
                in_specs=[SM, SM] + [VM] * 6,
                out_specs=(VM,) * (2 + first),
                scratch_shapes=scratch,
                input_output_aliases={6: first, 7: first + 1},
                compiler_params=PARAMS,
                cost_estimate=SHORT,
                name="backward",
            )
        )

    res = [[] for _ in range(CHUNKS)]
    own = None
    moving = [None] * CHUNKS
    blocks = [None] * CHUNKS
    cot = [None] * CHUNKS

    forward = [forward_call(c, False) for c in range(CHUNKS)]
    for step in range(segments - 1):
        for c in range(CHUNKS):
            passed = [] if own is None else [own]
            if step > 0:
                args = (at_step(step), info, moving[c], *weights, *passed)
                out, kept, own = forward[c](*args)
            else:
                args = (at_step(step), info, *weights, *passed)
                out, kept, own = forward_call(c, True)(*args)
            res[c].append(kept)
            moving[c] = exchange(out, "segment", neighbour_pairs(segments, step))
    for c in range(CHUNKS):
        out, kept, own, blocks[c], cot[c] = turn_call(c)(
            at_step(segments - 1), info, labels, moving[c], *weights, classifier.T, own
        )
        res[c].append(kept)
        moving[c] = exchange(out, "segment", neighbour_pairs(segments, segments - 2))

    def along_line(value, k):
        return exchange(value, "dp", [(i, i ^ (2 * k)) for i in range(replicas)])

    def again(ends, middles):
        lots = len(ends) * CHUNKS
        return pl.pallas_call(
            functools.partial(again_kernel, d, depth, len(ends), CHUNKS),
            out_shape=jax.ShapeDtypeStruct((4, lots * d.flat, feat), BF),
            in_specs=[SM, SM] + [VM] * 2 + [ANY] * (2 * len(ends)),
            out_specs=VM,
            scratch_shapes=[
                pltpu.VMEM((lots, 2) + packed, BF),
                pltpu.VMEM((lots * d.flat, feat), F32),
                scratch[0],
                scratch[0],
                scratch[1],
                scratch[2],
                pltpu.SemaphoreType.DMA((len(ends),)),
            ],
            compiler_params=WIDE if depth <= 4 else LONG_LINE,
            cost_estimate=SHORT,
            name="again",
        )(cell_count, (replica // 2).reshape(1), *weights, *ends, *middles)

    if depth == 4:
        middle = [(0, 1), (1, 0), (2, 4), (4, 2), (3, 5), (5, 3), (6, 7), (7, 6)]
        own, moving[0] = lax.optimization_barrier((own, moving[0]))
        beside = along_line(own, 1)
        across = exchange(own, "dp", middle)
        far = along_line(across, 1)
        across_far = exchange(beside, "dp", middle)
        outer = [(0, 6), (6, 0), (1, 7), (7, 1), (2, 3), (3, 2), (4, 5), (5, 4)]
        end_far = exchange(lax.optimization_barrier((own, beside))[0], "dp", outer)
        acts = [again([own, beside, far, end_far], [own, beside, across_far, across])]
    else:
        direct = [along_line(own, k) for k in range(1, depth)]
        acts = [again([own] + direct, [own] + direct)]

    backward, backward_end = backward_call(True), backward_call(False)
    for step in range(segments - 2, -1, -1):
        for c in range(CHUNKS):
            args = (at_step(step), info, moving[c], *weights, res[c][step], blocks[c], cot[c])
            if step > 0:
                out, blocks[c], cot[c] = backward(*args)
                moving[c] = exchange(out, "segment", neighbour_pairs(segments, step - 1))
            else:
                blocks[c], cot[c] = backward_end(*args)

    tap_rows = -(-slots * n_taps // 16) * 16
    total_rows = CHUNKS * slots * d.flat + tap_rows
    sent = pl.pallas_call(
        functools.partial(send_kernel, d, CHUNKS, n_taps, segments, depth),
        out_shape=(jax.ShapeDtypeStruct((total_rows, share), BF),) * depth,
        in_specs=[SM] + [VM] * (CHUNKS * (segments + 2)),
        out_specs=(VM,) * depth,
        scratch_shapes=[
            pltpu.VMEM((CHUNKS, 3) + packed, BF),
            pltpu.VMEM((depth, tap_rows, share), BF),
            pltpu.VMEM(packed, F32),
            pltpu.VMEM(packed, F32),
            pltpu.VMEM((d.tiles, tap_rows * SUB, LANE), F32),
        ],
        compiler_params=WIDE if depth <= 4 else LONG_LINE,
        cost_estimate=SHORT,
        name="send",
    )(info, *blocks, *[r for chunk in res for r in chunk], *cot)
    received = [sent[0]] + [along_line(sent[k], k) for k in range(1, depth)]

    sum_t = (4 * half + tap_rows, feat)
    mine, other = pl.pallas_call(
        functools.partial(product_kernel, d, CHUNKS, depth, len(acts)),
        out_shape=(jax.ShapeDtypeStruct(sum_t, F32), jax.ShapeDtypeStruct(sum_t, BF)),
        in_specs=[SM] + [VM] * (len(acts) + depth),
        out_specs=(VM, VM),
        compiler_params=WIDE if depth <= 4 else LONG_LINE,
        cost_estimate=SHORT,
        name="product",
    )(core, *acts, *received)
    swapped = exchange(other, "dp", [(i, i ^ 1) for i in range(replicas)])
    grad, three, five = pl.pallas_call(
        functools.partial(sum_kernel, d),
        out_shape=(
            jax.ShapeDtypeStruct((slots, 2, half, feat), F32),
            jax.ShapeDtypeStruct((n_three, slots, half), F32),
            jax.ShapeDtypeStruct((n_five, slots, half), F32),
        ),
        in_specs=[VM, VM],
        out_specs=(VM,) * 3,
        compiler_params=PARAMS,
        cost_estimate=SHORT,
        name="sum",
    )(mine, swapped)
    return (
        grad.transpose(0, 1, 3, 2),
        three.transpose(1, 0, 2),
        five.transpose(1, 0, 2),
    )


def solution(mesh):
    return jax.shard_map(
        per_device,
        mesh=mesh,
        in_specs=(
            P("dp", None, None, None),
            P("dp"),
            P("segment"),
            P("segment", None, None, None),
            P("segment", None, None),
            P("segment", None, None),
            P(),
        ),
        out_specs=(
            P("segment", None, None, "dp"),
            P("segment", None, "dp"),
            P("segment", None, "dp"),
        ),
        check_vma=False,
    )
```
